32 devices in a mesh: parts: 2 (over y), rows: 16 (over z, x, core).
Axes of the slice: x: 2, y: 2, z: 4, core: 2. Of those that a mesh axis runs over, the one named last changes fastest.
Arguments:
- features: bfloat16 [12288, 1024], P(('parts', 'rows')), parts along dimension 0, may hold values from -6 to 6
- w_self: bfloat16 [2, 1024, 1024], replicated, may hold values from -0.1875 to 0.1875
- w_neigh: bfloat16 [2, 1024, 1024], replicated, may hold values from -0.1875 to 0.1875
- requests: int32 [512, 8], P(('parts', 'rows')), parts along dimension 0, may hold values from 0 to 383
- counts: int32 [512], P(('parts', 'rows')), parts along dimension 0, may hold values from 0 to 8, as said below
- mask_remote: int32 [12288, 128], P(('parts', 'rows')), parts along dimension 0, may hold values 0 or 1
- mask_local: int32 [12288, 384], P(('parts', 'rows')), parts along dimension 0, may hold values 0 or 1
Outputs:
- embeddings: bfloat16 [12288, 1024], P(('parts', 'rows')), parts along dimension 0
The draws below stay inside these ranges and needn't reach their ends.
There are 2 independent parts, one for each index of `parts`. The reference program is written for one: setup_inputs(seed, part) draws one part's arguments, and reference() takes and returns one part's arrays. A program takes and returns all parts, laid end to end along the dimension named above; an argument that names none is the same for every part. Nothing has to cross between parts.
Inputs may be any that keep to these rules, and one draw needn't show every extreme that they name: `counts`: for each requesting device at least one owner's count is exactly 8.
All inputs are finite; a program needn't handle non-finite values. No bound on the sum of `mask_remote` or of `mask_local` on one device may be relied on, other than what follows from the above.
Results may differ from the reference program's by a relative error of at most 0.0047.
Values may be sent and summed in bfloat16 or wider, within the bound.
A program may use at most 64 MiB of HBM per device.

```python
import jax
import jax.numpy as jnp
from jax import lax

D = 1024
R_DEV = 384
SLOT = 8
LAYERS = 2
NODES = 6144
PAIRS = 256
FETCHED = 128
N_ROWS = 16


def draw_counts(key, part):
    key = jax.random.fold_in(key, 7)
    key_base, key_full = jax.random.split(key)
    base = jax.random.randint(key_base, (N_ROWS, N_ROWS), 0, SLOT + 1)
    full_owner = jax.random.randint(key_full, (N_ROWS, 1), 0, N_ROWS)
    owners = jnp.arange(N_ROWS, dtype=jnp.int32)[None, :]
    result = jnp.where(owners == full_owner, SLOT, base)
    return result.reshape(-1).astype(jnp.int32)


def place_ends(values, stream_key, least, largest):
    longest = values.shape.index(max(values.shape))
    spots = []
    for shift in (0, 1):
        where = [jax.random.randint(jax.random.fold_in(stream_key, axis), (), 0, length) for axis, length in enumerate(values.shape)]
        where[longest] = (where[longest] + shift) % values.shape[longest]
        spots.append(tuple(where))
    return values.at[spots[0]].set(least).at[spots[1]].set(largest)


def block_scale(key, shape, cuts, smallest, top_value):
    factor_of = 1.0
    for position, parts in cuts:
        draws = jax.random.uniform(jax.random.fold_in(jax.random.fold_in(key, 6), position), (parts,), jnp.float32, smallest / len(cuts), top_value / len(cuts))
        factor_of = factor_of * jnp.repeat(jnp.exp(draws), shape[position] // parts).reshape((-1,) + (1,) * (len(shape) - 1 - position))
    return factor_of


def gaussian(key, extent, deviation, bound, cuts=(), held_as=jnp.bfloat16):
    loudness = block_scale(key, extent, cuts, -0.22, 0.18) if cuts else 1.0
    array = jax.random.normal(key, extent, jnp.float32) * deviation * loudness
    return jnp.minimum(jnp.maximum(array, -bound), bound).astype(held_as)


def setup_inputs(seed: int = 0, part: int = 0) -> dict:
    streams_of = jax.random.split(jax.random.key(seed), 8)
    part_keys = jax.random.split(jax.random.fold_in(streams_of[7], part), 8)
    features = gaussian(part_keys[0], (NODES, D), 1.0, 6.0, ((0, 16),))
    w_self = gaussian(streams_of[1], (LAYERS, D, D), D ** -0.5, 0.1875)
    w_neigh = gaussian(streams_of[2], (LAYERS, D, D), D ** -0.5, 0.1875)
    requests = place_ends(jax.random.randint(part_keys[3], (PAIRS, SLOT), 0, R_DEV), jax.random.fold_in(part_keys[3], 1), 0, R_DEV - 1).astype(jnp.int32)
    counts = draw_counts(jax.random.fold_in(jax.random.fold_in(streams_of[7], part), 71), part)
    mask_remote = place_ends((jax.random.randint(part_keys[5], (NODES, FETCHED), 0, 32) < 1).astype(jnp.int32), jax.random.fold_in(part_keys[5], 1), 0, 1)
    mask_local = place_ends((jax.random.randint(part_keys[6], (NODES, R_DEV), 0, 32) < 1).astype(jnp.int32), jax.random.fold_in(part_keys[6], 1), 0, 1)
    return {"features": features, "w_self": w_self, "w_neigh": w_neigh, "requests": requests, "counts": counts, "mask_remote": mask_remote, "mask_local": mask_local}


def layer_step(h, weight_self, weight_neigh, requests, counts, mask_remote, mask_local):
    proj = jnp.dot(h, weight_neigh, preferred_element_type=jnp.float32).astype(jnp.bfloat16)
    self_part = jnp.dot(h, weight_self, preferred_element_type=jnp.float32)

    def one_owner(device):
        start = (device * R_DEV).astype(jnp.int32)
        own = lax.dynamic_slice_in_dim(proj, start, R_DEV, 0)
        wanted = lax.dynamic_slice_in_dim(requests, (device * N_ROWS).astype(jnp.int32), N_ROWS, 0)
        used = lax.dynamic_slice_in_dim(counts, (device * N_ROWS).astype(jnp.int32), N_ROWS, 0)
        owners = jnp.arange(N_ROWS, dtype=jnp.int32)[:, None] * R_DEV
        global_rows = (owners + wanted).reshape(-1)
        fetched = proj[global_rows]
        valid = (jnp.arange(SLOT, dtype=jnp.int32)[None, :] < used[:, None]).astype(jnp.int32).reshape(-1)
        remote = lax.dynamic_slice_in_dim(mask_remote, start, R_DEV, 0) * valid[None, :]
        local = lax.dynamic_slice_in_dim(mask_local, start, R_DEV, 0)
        degree = 1.0 + lax.optimization_barrier(jnp.sum(remote, axis=1)).astype(jnp.float32) + lax.optimization_barrier(jnp.sum(local, axis=1)).astype(jnp.float32)
        total = own.astype(jnp.float32)
        total = total + jnp.dot(local.astype(jnp.bfloat16), own, preferred_element_type=jnp.float32)
        total = total + jnp.dot(remote.astype(jnp.bfloat16), fetched, preferred_element_type=jnp.float32)
        return total / degree[:, None]
    mean_part = lax.map(one_owner, jnp.arange(N_ROWS, dtype=jnp.int32)).reshape(NODES, D)
    pre = self_part + mean_part
    act = jnp.maximum(pre, 0.0)
    scale = jnp.sqrt(lax.optimization_barrier(jnp.mean(act * act, axis=1, keepdims=True)) + 1e-05)
    return (act / scale).astype(jnp.bfloat16)

def reference(features, w_self, w_neigh, requests, counts, mask_remote, mask_local):
    h = features
    for layer in range(LAYERS):
        h = layer_step(h, w_self[layer], w_neigh[layer], requests, counts, mask_remote, mask_local)
    return h
```

```python
import functools

import jax
import jax.numpy as jnp
from jax import lax
from jax.experimental import pallas as pl
from jax.experimental.pallas import tpu as pltpu
from jax.sharding import PartitionSpec as P

LANES = 128
CHUNK = 256


def dot(a, b):
    return jnp.dot(a, b, preferred_element_type=jnp.float32)


def kernel(
    n, layers, feat_hbm, ws_hbm, wn_hbm, req_ref, cnt_ref, mr_hbm, ml_hbm, out_ref,
    hid, ws, wn, mr, ml, req_send, req_recv, row_send, row_recv,
    adj, edges, onehot, inv, base, local_sem, send_sem, recv_sem,
):
    me = lax.axis_index("rows")
    nodes, width = out_ref.shape
    slots = req_ref.shape[1]
    fetched = n * slots
    half = width // 2

    loads = [
        pltpu.make_async_copy(feat_hbm, hid, local_sem.at[0]),
        pltpu.make_async_copy(mr_hbm, mr, local_sem.at[1]),
        pltpu.make_async_copy(ml_hbm, ml, local_sem.at[2]),
    ]
    weights = []
    for layer in range(layers):
        weights.append((
            pltpu.make_async_copy(wn_hbm.at[layer], wn.at[layer], local_sem.at[3 + 2 * layer]),
            pltpu.make_async_copy(ws_hbm.at[layer], ws.at[layer], local_sem.at[4 + 2 * layer]),
        ))
    barrier = pltpu.get_barrier_semaphore()

    def greet(k, carry):
        peer = lax.rem(me + k, n)
        pl.semaphore_signal(
            barrier, inc=1, device_id={"rows": peer}, device_id_type=pl.DeviceIdType.MESH
        )
        return carry

    lax.fori_loop(1, n, greet, 0)
    for copy in loads:
        copy.start()
    for pair in weights:
        for copy in pair:
            copy.start()

    eye = lax.broadcasted_iota(jnp.int32, (slots, slots), 0) == lax.broadcasted_iota(
        jnp.int32, (slots, slots), 1
    )
    for o in range(n):
        row = jnp.broadcast_to(req_ref[o : o + 1, :], (slots, slots))
        column = jnp.sum(jnp.where(eye, row, 0), axis=1, keepdims=True)
        req_send[o] = jnp.broadcast_to(column, (slots, LANES))
    req_recv[me] = req_send[me]
    pl.semaphore_wait(barrier, n - 1)

    def remote(phase, src, dst, peer, origin):
        return pltpu.make_async_remote_copy(
            src_ref=src.at[peer],
            dst_ref=dst.at[origin],
            send_sem=send_sem.at[phase, peer],
            recv_sem=recv_sem.at[phase, origin],
            device_id={"rows": peer},
            device_id_type=pl.DeviceIdType.MESH,
        )

    def send_all(phase, src, dst):
        def body(k, carry):
            remote(phase, src, dst, lax.rem(me + k, n), me).start()
            return carry

        lax.fori_loop(1, n, body, 0)

    def recv_all(phase, src, dst):
        def body(k, carry):
            peer = lax.rem(me + k, n)
            remote(phase, src, dst, peer, peer).wait_recv()
            return carry

        lax.fori_loop(1, n, body, 0)

    def sent_all(phase, src, dst):
        def body(k, carry):
            remote(phase, src, dst, lax.rem(me + k, n), me).wait_send()
            return carry

        lax.fori_loop(1, n, body, 0)

    send_all(0, req_send, req_recv)

    lane = lax.broadcasted_iota(jnp.int32, (1, fetched), 1)
    owner = lane // slots
    used = jnp.zeros((1, fetched), jnp.int32)
    for o in range(n):
        used = jnp.where(owner == o, cnt_ref[o], used)
    valid = (lane - owner * slots < used).astype(jnp.int32)
    loads[1].wait()
    loads[2].wait()
    remote_int = mr[...] * valid
    local_int = ml[...]
    edges[...] = remote_int.astype(jnp.float32).astype(jnp.bfloat16)
    diagonal = lax.broadcasted_iota(jnp.int32, (nodes, nodes), 0) == lax.broadcasted_iota(
        jnp.int32, (nodes, nodes), 1
    )
    adj[...] = (
        (local_int + diagonal.astype(jnp.int32)).astype(jnp.float32).astype(jnp.bfloat16)
    )
    degree = 1.0 + (
        jnp.sum(remote_int.astype(jnp.float32), axis=1, keepdims=True)
        + jnp.sum(local_int.astype(jnp.float32), axis=1, keepdims=True)
    )
    inv[...] = jnp.broadcast_to(1.0 / degree, (nodes, LANES))

    loads[0].wait()
    recv_all(0, req_send, req_recv)
    wanted = req_recv[...].reshape(fetched, LANES)
    lanes = lax.broadcasted_iota(jnp.int32, (fetched, LANES), 1)
    for c in range(nodes // LANES):
        onehot[:, c * LANES : (c + 1) * LANES] = (
            (wanted == lanes + c * LANES).astype(jnp.float32).astype(jnp.bfloat16)
        )

    for layer in range(layers):
        src, dst = row_send.at[layer], row_recv.at[layer]
        for part in range(2):
            picked = dot(onehot[...], hid[:, part * half : (part + 1) * half])
            for_peers = picked.reshape(n, slots, half)
            if part == 0:
                first = for_peers
            else:
                both = jnp.concatenate([first, for_peers], axis=1)
                row_send[layer] = both.astype(jnp.bfloat16)
        row_recv[layer, me] = row_send[layer, me]
        send_all(1 + layer, src, dst)

        for copy in weights[layer]:
            copy.wait()
        scale = jnp.concatenate([inv[...]] * (CHUNK // LANES), axis=1)
        for c in range(width // CHUNK):
            cols = slice(c * CHUNK, (c + 1) * CHUNK)
            proj = dot(hid[...], wn[layer, :, cols]).astype(jnp.bfloat16)
            base[:, cols] = dot(hid[...], ws[layer, :, cols]) + dot(adj[...], proj) * scale

        recv_all(1 + layer, src, dst)
        block = row_recv[layer].astype(jnp.float32)
        rows = jnp.concatenate(
            [block[:, :slots, :].reshape(fetched, half), block[:, slots:, :].reshape(fetched, half)],
            axis=1,
        ).astype(jnp.bfloat16)
        squares = jnp.zeros((nodes, LANES), jnp.float32)
        for c in range(width // CHUNK):
            cols = slice(c * CHUNK, (c + 1) * CHUNK)
            proj = dot(rows, wn[layer, :, cols]).astype(jnp.bfloat16)
            act = jnp.maximum(base[:, cols] + dot(edges[...], proj) * scale, 0.0)
            base[:, cols] = act
            for part in range(CHUNK // LANES):
                piece = act[:, part * LANES : (part + 1) * LANES]
                squares = squares + piece * piece
        mean = jnp.sum(squares, axis=1, keepdims=True) * (1.0 / width)
        norm = lax.rsqrt(mean + 1e-05)
        result = out_ref if layer == layers - 1 else hid
        for c in range(width // CHUNK):
            cols = slice(c * CHUNK, (c + 1) * CHUNK)
            result[:, cols] = (base[:, cols] * norm).astype(jnp.bfloat16)

    sent_all(0, req_send, req_recv)
    for layer in range(layers):
        sent_all(1 + layer, row_send.at[layer], row_recv.at[layer])


def shards(features, w_self, w_neigh, requests, counts, mask_remote, mask_local):
    n = lax.axis_size("rows")
    nodes, width = features.shape
    layers = w_self.shape[0]
    slots = requests.shape[1]
    fetched = n * slots
    flops = 2 * layers * nodes * width * (2 * width + nodes + fetched)
    hbm = pl.BlockSpec(memory_space=pl.ANY)
    return pl.pallas_call(
        functools.partial(kernel, n, layers),
        out_shape=jax.ShapeDtypeStruct((nodes, width), jnp.bfloat16),
        in_specs=[
            hbm, hbm, hbm,
            pl.BlockSpec(memory_space=pltpu.VMEM),
            pl.BlockSpec(memory_space=pltpu.SMEM),
            hbm, hbm,
        ],
        out_specs=pl.BlockSpec(memory_space=pltpu.VMEM),
        scratch_shapes=[
            pltpu.VMEM((nodes, width), jnp.bfloat16),
            pltpu.VMEM(w_self.shape, jnp.bfloat16),
            pltpu.VMEM(w_neigh.shape, jnp.bfloat16),
            pltpu.VMEM(mask_remote.shape, jnp.int32),
            pltpu.VMEM(mask_local.shape, jnp.int32),
            pltpu.VMEM((n, slots, LANES), jnp.int32),
            pltpu.VMEM((n, slots, LANES), jnp.int32),
            pltpu.VMEM((layers, n, 2 * slots, width // 2), jnp.bfloat16),
            pltpu.VMEM((layers, n, 2 * slots, width // 2), jnp.bfloat16),
            pltpu.VMEM((nodes, nodes), jnp.bfloat16),
            pltpu.VMEM((nodes, fetched), jnp.bfloat16),
            pltpu.VMEM((fetched, nodes), jnp.bfloat16),
            pltpu.VMEM((nodes, LANES), jnp.float32),
            pltpu.VMEM((nodes, width), jnp.float32),
            pltpu.SemaphoreType.DMA((3 + 2 * layers,)),
            pltpu.SemaphoreType.DMA((1 + layers, n)),
            pltpu.SemaphoreType.DMA((1 + layers, n)),
        ],
        compiler_params=pltpu.CompilerParams(
            collective_id=0, has_side_effects=True, vmem_limit_bytes=52 * 1024 * 1024
        ),
        cost_estimate=pl.CostEstimate(
            flops=flops, bytes_accessed=8 * width * width + 4 * nodes * width, transcendentals=0
        ),
    )(features, w_self, w_neigh, requests, counts, mask_remote, mask_local)


def solution(mesh):
    in_specs = (
        P(("parts", "rows"), None),
        P(),
        P(),
        P(("parts", "rows"), None),
        P(("parts", "rows")),
        P(("parts", "rows"), None),
        P(("parts", "rows"), None),
    )
    out_specs = P(("parts", "rows"), None)
    return jax.shard_map(shards, mesh=mesh, in_specs=in_specs, out_specs=out_specs, check_vma=False)
```

```python
import functools

import jax
import jax.numpy as jnp
from jax import lax
from jax.experimental import pallas as pl
from jax.experimental.pallas import tpu as pltpu
from jax.sharding import PartitionSpec as P

LANES = 128
CHUNK = 256


def dot(a, b):
    return jnp.dot(a, b, preferred_element_type=jnp.float32)


def kernel(
    n, layers, feat_hbm, ws_hbm, wn_hbm, req_hbm, cnt_hbm, mr_hbm, ml_hbm, out_ref,
    req_ref, cnt_ref, hid, ws, wn, mr, ml, req_send, req_recv, row_send, row_recv,
    adj, edges, onehot, inv, base, local_sem, send_sem, recv_sem,
):
    me = lax.axis_index("rows")
    nodes, width = out_ref.shape
    slots = req_ref.shape[0]
    fetched = n * slots
    half = width // 2
    unroll = n <= 16

    loads = [
        pltpu.make_async_copy(req_hbm, req_ref, local_sem.at[0]),
        pltpu.make_async_copy(cnt_hbm, cnt_ref, local_sem.at[1]),
        pltpu.make_async_copy(mr_hbm, mr, local_sem.at[2]),
        pltpu.make_async_copy(ml_hbm, ml, local_sem.at[3]),
        pltpu.make_async_copy(feat_hbm, hid, local_sem.at[4]),
    ]
    weights = []
    for layer in range(layers):
        weights.append((
            pltpu.make_async_copy(wn_hbm.at[layer], wn.at[layer], local_sem.at[5 + 2 * layer]),
            pltpu.make_async_copy(ws_hbm.at[layer], ws.at[layer], local_sem.at[6 + 2 * layer]),
        ))
    barrier = pltpu.get_barrier_semaphore()

    def greet(k, carry):
        peer = lax.rem(me + k, n)
        pl.semaphore_signal(
            barrier, inc=1, device_id={"rows": peer}, device_id_type=pl.DeviceIdType.MESH
        )
        return carry

    lax.fori_loop(1, n, greet, 0, unroll=unroll)
    for copy in loads:
        copy.start()
    for pair in weights:
        for copy in pair:
            copy.start()

    loads[0].wait()
    for o in range(n):
        req_send[o] = jnp.broadcast_to(req_ref[:, o : o + 1], (slots, LANES))
    req_recv[me] = req_send[me]
    pl.semaphore_wait(barrier, n - 1)

    def remote(phase, src, dst, peer, origin):
        return pltpu.make_async_remote_copy(
            src_ref=src.at[peer],
            dst_ref=dst.at[origin],
            send_sem=send_sem.at[phase, peer],
            recv_sem=recv_sem.at[phase, origin],
            device_id={"rows": peer},
            device_id_type=pl.DeviceIdType.MESH,
        )

    def send_all(phase, src, dst):
        def body(k, carry):
            remote(phase, src, dst, lax.rem(me + k, n), me).start()
            return carry

        lax.fori_loop(1, n, body, 0, unroll=unroll)

    def recv_all(phase, src, dst):
        def body(k, carry):
            peer = lax.rem(me + k, n)
            remote(phase, src, dst, peer, peer).wait_recv()
            return carry

        lax.fori_loop(1, n, body, 0, unroll=unroll)

    def sent_all(phase, src, dst):
        def body(k, carry):
            remote(phase, src, dst, lax.rem(me + k, n), me).wait_send()
            return carry

        lax.fori_loop(1, n, body, 0, unroll=unroll)

    send_all(0, req_send, req_recv)

    lane = lax.broadcasted_iota(jnp.int32, (1, fetched), 1)
    owner = lane // slots
    loads[1].wait()
    used = jnp.zeros((1, fetched), jnp.int32)
    for o in range(n):
        used = jnp.where(owner == o, cnt_ref[o], used)
    valid = (lane - owner * slots < used).astype(jnp.int32)
    loads[2].wait()
    loads[3].wait()
    remote_int = mr[...] * valid
    local_int = ml[...]
    edges[...] = remote_int.astype(jnp.float32).astype(jnp.bfloat16)
    diagonal = lax.broadcasted_iota(jnp.int32, (nodes, nodes), 0) == lax.broadcasted_iota(
        jnp.int32, (nodes, nodes), 1
    )
    adj[...] = (
        (local_int + diagonal.astype(jnp.int32)).astype(jnp.float32).astype(jnp.bfloat16)
    )
    degree = 1.0 + (
        jnp.sum(remote_int.astype(jnp.float32), axis=1, keepdims=True)
        + jnp.sum(local_int.astype(jnp.float32), axis=1, keepdims=True)
    )
    inv[...] = jnp.broadcast_to(1.0 / degree, (nodes, LANES))

    loads[4].wait()
    recv_all(0, req_send, req_recv)
    wanted = req_recv[...].reshape(fetched, LANES)
    lanes = lax.broadcasted_iota(jnp.int32, (fetched, LANES), 1)
    for c in range(nodes // LANES):
        onehot[:, c * LANES : (c + 1) * LANES] = (
            (wanted == lanes + c * LANES).astype(jnp.float32).astype(jnp.bfloat16)
        )

    for layer in range(layers):
        src, dst = row_send.at[layer], row_recv.at[layer]
        for part in range(2):
            picked = dot(onehot[...], hid[:, part * half : (part + 1) * half])
            for_peers = picked.reshape(n, slots, half)
            if part == 0:
                first = for_peers
            else:
                both = jnp.concatenate([first, for_peers], axis=1)
                row_send[layer] = both.astype(jnp.bfloat16)
        row_recv[layer, me] = row_send[layer, me]
        send_all(1 + layer, src, dst)

        for copy in weights[layer]:
            copy.wait()
        scale = jnp.concatenate([inv[...]] * (CHUNK // LANES), axis=1)
        for c in range(width // CHUNK):
            cols = slice(c * CHUNK, (c + 1) * CHUNK)
            proj = dot(hid[...], wn[layer, :, cols]).astype(jnp.bfloat16)
            base[:, cols] = dot(hid[...], ws[layer, :, cols]) + dot(adj[...], proj) * scale

        recv_all(1 + layer, src, dst)
        block = row_recv[layer].astype(jnp.float32)
        rows = jnp.concatenate(
            [block[:, :slots, :].reshape(fetched, half), block[:, slots:, :].reshape(fetched, half)],
            axis=1,
        ).astype(jnp.bfloat16)
        squares = jnp.zeros((nodes, LANES), jnp.float32)
        for c in range(width // CHUNK):
            cols = slice(c * CHUNK, (c + 1) * CHUNK)
            proj = dot(rows, wn[layer, :, cols]).astype(jnp.bfloat16)
            act = jnp.maximum(base[:, cols] + dot(edges[...], proj) * scale, 0.0)
            base[:, cols] = act
            for part in range(CHUNK // LANES):
                piece = act[:, part * LANES : (part + 1) * LANES]
                squares = squares + piece * piece
        mean = jnp.sum(squares, axis=1, keepdims=True) * (1.0 / width)
        norm = lax.rsqrt(mean + 1e-05)
        result = out_ref if layer == layers - 1 else hid
        for c in range(width // CHUNK):
            cols = slice(c * CHUNK, (c + 1) * CHUNK)
            result[:, cols] = (base[:, cols] * norm).astype(jnp.bfloat16)

    sent_all(0, req_send, req_recv)
    for layer in range(layers):
        sent_all(1 + layer, row_send.at[layer], row_recv.at[layer])


def shards(features, w_self, w_neigh, requests, counts, mask_remote, mask_local):
    n = lax.axis_size("rows")
    nodes, width = features.shape
    layers = w_self.shape[0]
    slots = requests.shape[1]
    fetched = n * slots
    flops = 2 * layers * nodes * width * (2 * width + nodes + fetched)
    hbm = pl.BlockSpec(memory_space=pltpu.HBM)
    return pl.pallas_call(
        functools.partial(kernel, n, layers),
        out_shape=pltpu.VMEM((nodes, width), jnp.bfloat16),
        in_specs=[hbm] * 7,
        out_specs=pl.BlockSpec(memory_space=pltpu.VMEM),
        scratch_shapes=[
            pltpu.VMEM((slots, n), jnp.int32),
            pltpu.SMEM(counts.shape, jnp.int32),
            pltpu.VMEM((nodes, width), jnp.bfloat16),
            pltpu.VMEM(w_self.shape, jnp.bfloat16),
            pltpu.VMEM(w_neigh.shape, jnp.bfloat16),
            pltpu.VMEM(mask_remote.shape, jnp.int32),
            pltpu.VMEM(mask_local.shape, jnp.int32),
            pltpu.VMEM((n, slots, LANES), jnp.int32),
            pltpu.VMEM((n, slots, LANES), jnp.int32),
            pltpu.VMEM((layers, n, 2 * slots, width // 2), jnp.bfloat16),
            pltpu.VMEM((layers, n, 2 * slots, width // 2), jnp.bfloat16),
            pltpu.VMEM((nodes, nodes), jnp.bfloat16),
            pltpu.VMEM((nodes, fetched), jnp.bfloat16),
            pltpu.VMEM((fetched, nodes), jnp.bfloat16),
            pltpu.VMEM((nodes, LANES), jnp.float32),
            pltpu.VMEM((nodes, width), jnp.float32),
            pltpu.SemaphoreType.DMA((5 + 2 * layers,)),
            pltpu.SemaphoreType.DMA((1 + layers, n)),
            pltpu.SemaphoreType.DMA((1 + layers, n)),
        ],
        compiler_params=pltpu.CompilerParams(
            collective_id=0, has_side_effects=True, vmem_limit_bytes=56 * 1024 * 1024
        ),
        cost_estimate=pl.CostEstimate(
            flops=flops, bytes_accessed=8 * width * width + 4 * nodes * width, transcendentals=0
        ),
    )(features, w_self, w_neigh, requests.T, counts, mask_remote, mask_local)


def solution(mesh):
    in_specs = (
        P(("parts", "rows"), None),
        P(),
        P(),
        P(("parts", "rows"), None),
        P(("parts", "rows")),
        P(("parts", "rows"), None),
        P(("parts", "rows"), None),
    )
    out_specs = P(("parts", "rows"), None)
    return jax.shard_map(shards, mesh=mesh, in_specs=in_specs, out_specs=out_specs, check_vma=False)
```

```python
import functools

import jax
import jax.numpy as jnp
from jax import lax
from jax.experimental import pallas as pl
from jax.experimental.pallas import tpu as pltpu
from jax.sharding import PartitionSpec as P

LANES = 128
CHUNK = 512


def dot(a, b):
    return jnp.dot(a, b, preferred_element_type=jnp.float32)


def kernel(
    n, layers, feat_hbm, ws_hbm, wn_hbm, req_hbm, cnt_hbm, mr_hbm, ml_hbm, out_ref,
    req_ref, cnt_ref, hid, ws, wn, mr, ml, req_send, req_recv, row_send, row_recv,
    adj, edges, onehot, inv, base, raw, local_sem, send_sem, recv_sem,
):
    me = lax.axis_index("rows")
    nodes, width = out_ref.shape
    slots = req_ref.shape[0]
    fetched = n * slots
    half = width // 2
    unroll = n <= 16

    loads = [
        pltpu.make_async_copy(req_hbm, req_ref, local_sem.at[0]),
        pltpu.make_async_copy(cnt_hbm, cnt_ref, local_sem.at[1]),
        pltpu.make_async_copy(mr_hbm, mr, local_sem.at[2]),
        pltpu.make_async_copy(ml_hbm, ml, local_sem.at[3]),
        pltpu.make_async_copy(feat_hbm, hid, local_sem.at[4]),
    ]
    weights = []
    for layer in range(layers):
        weights.append((
            pltpu.make_async_copy(wn_hbm.at[layer], wn.at[layer], local_sem.at[5 + 2 * layer]),
            pltpu.make_async_copy(ws_hbm.at[layer], ws.at[layer], local_sem.at[6 + 2 * layer]),
        ))
    barrier = pltpu.get_barrier_semaphore()

    def greet(k, carry):
        peer = lax.rem(me + k, n)
        pl.semaphore_signal(
            barrier, inc=1, device_id={"rows": peer}, device_id_type=pl.DeviceIdType.MESH
        )
        return carry

    lax.fori_loop(1, n, greet, 0, unroll=unroll)
    for copy in loads:
        copy.start()
    for pair in weights:
        for copy in pair:
            copy.start()

    diag = lax.broadcasted_iota(jnp.int32, (slots, LANES), 0) == lax.broadcasted_iota(
        jnp.int32, (slots, LANES), 1
    )
    loads[0].wait()
    for o in range(n):
        column = jnp.broadcast_to(req_ref[:, o : o + 1], (slots, LANES))
        req_send[o] = jnp.sum(jnp.where(diag, column, 0), axis=0, keepdims=True)
    req_recv[me] = req_send[me]
    pl.semaphore_wait(barrier, n - 1)

    def remote(phase, src, dst, peer, origin):
        return pltpu.make_async_remote_copy(
            src_ref=src.at[peer],
            dst_ref=dst.at[origin],
            send_sem=send_sem.at[phase, peer],
            recv_sem=recv_sem.at[phase, origin],
            device_id={"rows": peer},
            device_id_type=pl.DeviceIdType.MESH,
        )

    def send_all(phase, src, dst):
        def body(k, carry):
            remote(phase, src, dst, lax.rem(me + k, n), me).start()
            return carry

        lax.fori_loop(1, n, body, 0, unroll=unroll)

    def recv_all(phase, src, dst):
        def body(k, carry):
            peer = lax.rem(me + k, n)
            remote(phase, src, dst, peer, peer).wait_recv()
            return carry

        lax.fori_loop(1, n, body, 0, unroll=unroll)

    def sent_all(phase, src, dst):
        def body(k, carry):
            remote(phase, src, dst, lax.rem(me + k, n), me).wait_send()
            return carry

        lax.fori_loop(1, n, body, 0, unroll=unroll)

    send_all(0, req_send, req_recv)

    lane = lax.broadcasted_iota(jnp.int32, (1, fetched), 1)
    owner = lane // slots
    loads[1].wait()
    used = jnp.zeros((1, fetched), jnp.int32)
    for o in range(n):
        used = jnp.where(owner == o, cnt_ref[o], used)
    valid = (lane - owner * slots < used).astype(jnp.int32)
    loads[2].wait()
    loads[3].wait()
    remote_int = mr[...] * valid
    local_int = ml[...]
    edges[...] = remote_int.astype(jnp.float32).astype(jnp.bfloat16)
    diagonal = lax.broadcasted_iota(jnp.int32, (nodes, nodes), 0) == lax.broadcasted_iota(
        jnp.int32, (nodes, nodes), 1
    )
    adj[...] = (
        (local_int + diagonal.astype(jnp.int32)).astype(jnp.float32).astype(jnp.bfloat16)
    )
    degree = 1.0 + (
        jnp.sum(remote_int.astype(jnp.float32), axis=1, keepdims=True)
        + jnp.sum(local_int.astype(jnp.float32), axis=1, keepdims=True)
    )
    inv[...] = jnp.broadcast_to(1.0 / degree, (nodes, LANES))

    loads[4].wait()
    recv_all(0, req_send, req_recv)
    spread = jnp.broadcast_to(req_recv[...], (n, slots, LANES))
    columns = jnp.sum(jnp.where(diag[None], spread, 0), axis=2, keepdims=True)
    wanted = jnp.broadcast_to(columns, (n, slots, LANES)).reshape(fetched, LANES)
    lanes = lax.broadcasted_iota(jnp.int32, (fetched, LANES), 1)
    for c in range(nodes // LANES):
        onehot[:, c * LANES : (c + 1) * LANES] = (
            (wanted == lanes + c * LANES).astype(jnp.float32).astype(jnp.bfloat16)
        )

    def send_rows(source, layer):
        pieces = []
        for part in range(2):
            picked = dot(onehot[...], source[:, part * half : (part + 1) * half])
            pieces.append(picked.reshape(n, slots, half))
        row_send[layer] = jnp.concatenate(pieces, axis=1).astype(jnp.bfloat16)
        row_recv[layer, me] = row_send[layer, me]
        send_all(1 + layer, row_send.at[layer], row_recv.at[layer])

    send_rows(hid, 0)
    for layer in range(layers):
        src, dst = row_send.at[layer], row_recv.at[layer]
        for copy in weights[layer]:
            copy.wait()
        scale = jnp.concatenate([inv[...]] * (CHUNK // LANES), axis=1)
        for c in range(width // CHUNK):
            cols = slice(c * CHUNK, (c + 1) * CHUNK)
            proj = dot(hid[...], wn[layer, :, cols]).astype(jnp.bfloat16)
            base[:, cols] = dot(hid[...], ws[layer, :, cols]) + dot(adj[...], proj) * scale

        recv_all(1 + layer, src, dst)
        block = row_recv[layer].astype(jnp.float32)
        rows = jnp.concatenate(
            [block[:, :slots, :].reshape(fetched, half), block[:, slots:, :].reshape(fetched, half)],
            axis=1,
        )
        if layer > 0:
            row_mean = jnp.sum(rows * rows, axis=1, keepdims=True) * (1.0 / width)
            row_norm = lax.rsqrt(row_mean + 1e-05)
        rows = rows.astype(jnp.bfloat16)
        squares = jnp.zeros((nodes, LANES), jnp.float32)
        for c in range(width // CHUNK):
            cols = slice(c * CHUNK, (c + 1) * CHUNK)
            proj = dot(rows, wn[layer, :, cols])
            if layer > 0:
                proj = proj * row_norm
            proj = proj.astype(jnp.bfloat16)
            act = jnp.maximum(base[:, cols] + dot(edges[...], proj) * scale, 0.0)
            base[:, cols] = act
            if layer < layers - 1:
                raw[:, cols] = act.astype(jnp.bfloat16)
            for part in range(CHUNK // LANES):
                piece = act[:, part * LANES : (part + 1) * LANES]
                squares = squares + piece * piece
        if layer < layers - 1:
            send_rows(raw, layer + 1)
        mean = jnp.sum(squares, axis=1, keepdims=True) * (1.0 / width)
        norm = lax.rsqrt(mean + 1e-05)
        result = out_ref if layer == layers - 1 else hid
        for c in range(width // CHUNK):
            cols = slice(c * CHUNK, (c + 1) * CHUNK)
            result[:, cols] = (base[:, cols] * norm).astype(jnp.bfloat16)

    sent_all(0, req_send, req_recv)
    for layer in range(layers):
        sent_all(1 + layer, row_send.at[layer], row_recv.at[layer])


def shards(features, w_self, w_neigh, requests, counts, mask_remote, mask_local):
    n = lax.axis_size("rows")
    nodes, width = features.shape
    layers = w_self.shape[0]
    slots = requests.shape[1]
    fetched = n * slots
    flops = 2 * layers * nodes * width * (2 * width + nodes + fetched)
    hbm = pl.BlockSpec(memory_space=pltpu.HBM)
    return pl.pallas_call(
        functools.partial(kernel, n, layers),
        out_shape=pltpu.VMEM((nodes, width), jnp.bfloat16),
        in_specs=[hbm] * 7,
        out_specs=pl.BlockSpec(memory_space=pltpu.VMEM),
        scratch_shapes=[
            pltpu.VMEM((slots, n), jnp.int32),
            pltpu.SMEM(counts.shape, jnp.int32),
            pltpu.VMEM((nodes, width), jnp.bfloat16),
            pltpu.VMEM(w_self.shape, jnp.bfloat16),
            pltpu.VMEM(w_neigh.shape, jnp.bfloat16),
            pltpu.VMEM(mask_remote.shape, jnp.int32),
            pltpu.VMEM(mask_local.shape, jnp.int32),
            pltpu.VMEM((n, 1, LANES), jnp.int32),
            pltpu.VMEM((n, 1, LANES), jnp.int32),
            pltpu.VMEM((layers, n, 2 * slots, width // 2), jnp.bfloat16),
            pltpu.VMEM((layers, n, 2 * slots, width // 2), jnp.bfloat16),
            pltpu.VMEM((nodes, nodes), jnp.bfloat16),
            pltpu.VMEM((nodes, fetched), jnp.bfloat16),
            pltpu.VMEM((fetched, nodes), jnp.bfloat16),
            pltpu.VMEM((nodes, LANES), jnp.float32),
            pltpu.VMEM((nodes, width), jnp.float32),
            pltpu.VMEM((nodes, width), jnp.bfloat16),
            pltpu.SemaphoreType.DMA((5 + 2 * layers,)),
            pltpu.SemaphoreType.DMA((1 + layers, n)),
            pltpu.SemaphoreType.DMA((1 + layers, n)),
        ],
        compiler_params=pltpu.CompilerParams(
            collective_id=0, has_side_effects=True, vmem_limit_bytes=56 * 1024 * 1024
        ),
        cost_estimate=pl.CostEstimate(
            flops=flops, bytes_accessed=8 * width * width + 4 * nodes * width, transcendentals=0
        ),
    )(features, w_self, w_neigh, requests.T, counts, mask_remote, mask_local)


def solution(mesh):
    in_specs = (
        P(("parts", "rows"), None),
        P(),
        P(),
        P(("parts", "rows"), None),
        P(("parts", "rows")),
        P(("parts", "rows"), None),
        P(("parts", "rows"), None),
    )
    out_specs = P(("parts", "rows"), None)
    return jax.shard_map(shards, mesh=mesh, in_specs=in_specs, out_specs=out_specs, check_vma=False)
```

```python
import functools

import jax
import jax.numpy as jnp
from jax import lax
from jax.experimental import pallas as pl
from jax.experimental.pallas import tpu as pltpu
from jax.sharding import PartitionSpec as P

LANES = 128
CHUNK = 512


def dot(a, b):
    return jnp.dot(a, b, preferred_element_type=jnp.float32)


def kernel(
    n, layers, feat_hbm, ws_hbm, wn_hbm, req_hbm, cnt_hbm, mr_hbm, ml_hbm, out_ref,
    req_ref, cnt_ref, hid, ws, wn, mr, ml, req_send, req_recv, row_send, row_recv,
    adj, edges, onehot, inv, base, raw, local_sem, send_sem, recv_sem,
):
    me = lax.axis_index("rows")
    nodes, width = out_ref.shape
    slots = req_ref.shape[0]
    fetched = n * slots
    half = width // 2
    unroll = n <= 16

    loads = [
        pltpu.make_async_copy(req_hbm, req_ref, local_sem.at[0]),
        pltpu.make_async_copy(cnt_hbm, cnt_ref, local_sem.at[1]),
        pltpu.make_async_copy(mr_hbm, mr, local_sem.at[2]),
        pltpu.make_async_copy(ml_hbm, ml, local_sem.at[3]),
        pltpu.make_async_copy(feat_hbm, hid, local_sem.at[4]),
    ]
    weights = []
    for layer in range(layers):
        weights.append((
            pltpu.make_async_copy(wn_hbm.at[layer], wn.at[layer], local_sem.at[5 + 2 * layer]),
            pltpu.make_async_copy(ws_hbm.at[layer], ws.at[layer], local_sem.at[6 + 2 * layer]),
        ))
    barrier = pltpu.get_barrier_semaphore()

    def greet(k, carry):
        peer = lax.rem(me + k, n)
        pl.semaphore_signal(
            barrier, inc=1, device_id={"rows": peer}, device_id_type=pl.DeviceIdType.MESH
        )
        return carry

    lax.fori_loop(1, n, greet, 0, unroll=unroll)
    for copy in loads:
        copy.start()
    for pair in weights:
        for copy in pair:
            copy.start()

    diag = lax.broadcasted_iota(jnp.int32, (slots, LANES), 0) == lax.broadcasted_iota(
        jnp.int32, (slots, LANES), 1
    )
    loads[0].wait()
    for o in range(n):
        column = jnp.broadcast_to(req_ref[:, o : o + 1], (slots, LANES))
        req_send[o] = jnp.sum(jnp.where(diag, column, 0), axis=0, keepdims=True)
    req_recv[me] = req_send[me]
    lane = lax.broadcasted_iota(jnp.int32, (1, fetched), 1)
    owner = lane // slots
    loads[1].wait()
    used = jnp.zeros((1, fetched), jnp.int32)
    for o in range(n):
        used = jnp.where(owner == o, cnt_ref[o], used)
    valid = (lane - owner * slots < used).astype(jnp.int32)
    loads[2].wait()
    loads[3].wait()
    remote_int = mr[...] * valid
    local_int = ml[...]
    edges[...] = remote_int.astype(jnp.float32).astype(jnp.bfloat16)
    diagonal = lax.broadcasted_iota(jnp.int32, (nodes, nodes), 0) == lax.broadcasted_iota(
        jnp.int32, (nodes, nodes), 1
    )
    adj[...] = (
        (local_int + diagonal.astype(jnp.int32)).astype(jnp.float32).astype(jnp.bfloat16)
    )
    degree = 1.0 + (
        jnp.sum(remote_int.astype(jnp.float32), axis=1, keepdims=True)
        + jnp.sum(local_int.astype(jnp.float32), axis=1, keepdims=True)
    )
    inv[...] = jnp.broadcast_to(1.0 / degree, (nodes, LANES))

    pl.semaphore_wait(barrier, n - 1)

    def remote(phase, src, dst, peer, origin):
        return pltpu.make_async_remote_copy(
            src_ref=src.at[peer],
            dst_ref=dst.at[origin],
            send_sem=send_sem.at[phase, peer],
            recv_sem=recv_sem.at[phase, origin],
            device_id={"rows": peer},
            device_id_type=pl.DeviceIdType.MESH,
        )

    def send_all(phase, src, dst):
        def body(k, carry):
            remote(phase, src, dst, lax.rem(me + k, n), me).start()
            return carry

        lax.fori_loop(1, n, body, 0, unroll=unroll)

    def recv_all(phase, src, dst):
        def body(k, carry):
            peer = lax.rem(me + k, n)
            remote(phase, src, dst, peer, peer).wait_recv()
            return carry

        lax.fori_loop(1, n, body, 0, unroll=unroll)

    def sent_all(phase, src, dst):
        def body(k, carry):
            remote(phase, src, dst, lax.rem(me + k, n), me).wait_send()
            return carry

        lax.fori_loop(1, n, body, 0, unroll=unroll)

    send_all(0, req_send, req_recv)

    loads[4].wait()
    recv_all(0, req_send, req_recv)
    spread = jnp.broadcast_to(req_recv[...], (n, slots, LANES))
    columns = jnp.sum(jnp.where(diag[None], spread, 0), axis=2, keepdims=True)
    wanted = jnp.broadcast_to(columns, (n, slots, LANES)).reshape(fetched, LANES)
    lanes = lax.broadcasted_iota(jnp.int32, (fetched, LANES), 1)
    for c in range(nodes // LANES):
        onehot[:, c * LANES : (c + 1) * LANES] = (
            (wanted == lanes + c * LANES).astype(jnp.float32).astype(jnp.bfloat16)
        )

    def send_rows(source, layer):
        pieces = []
        for part in range(2):
            picked = dot(onehot[...], source[:, part * half : (part + 1) * half])
            pieces.append(picked.reshape(n, slots, half))
        row_send[layer] = jnp.concatenate(pieces, axis=1).astype(jnp.bfloat16)
        row_recv[layer, me] = row_send[layer, me]
        send_all(1 + layer, row_send.at[layer], row_recv.at[layer])

    send_rows(hid, 0)
    for layer in range(layers):
        src, dst = row_send.at[layer], row_recv.at[layer]
        for copy in weights[layer]:
            copy.wait()
        scale = jnp.concatenate([inv[...]] * (CHUNK // LANES), axis=1)
        for c in range(width // CHUNK):
            cols = slice(c * CHUNK, (c + 1) * CHUNK)
            proj = dot(hid[...], wn[layer, :, cols]).astype(jnp.bfloat16)
            base[:, cols] = dot(hid[...], ws[layer, :, cols]) + dot(adj[...], proj) * scale

        recv_all(1 + layer, src, dst)
        block = row_recv[layer].astype(jnp.float32)
        rows = jnp.concatenate(
            [block[:, :slots, :].reshape(fetched, half), block[:, slots:, :].reshape(fetched, half)],
            axis=1,
        )
        if layer > 0:
            row_mean = jnp.sum(rows * rows, axis=1, keepdims=True) * (1.0 / width)
            row_norm = lax.rsqrt(row_mean + 1e-05)
        rows = rows.astype(jnp.bfloat16)
        squares = jnp.zeros((nodes, LANES), jnp.float32)
        for c in range(width // CHUNK):
            cols = slice(c * CHUNK, (c + 1) * CHUNK)
            proj = dot(rows, wn[layer, :, cols])
            if layer > 0:
                proj = proj * row_norm
            proj = proj.astype(jnp.bfloat16)
            act = jnp.maximum(base[:, cols] + dot(edges[...], proj) * scale, 0.0)
            base[:, cols] = act
            if layer < layers - 1:
                raw[:, cols] = act.astype(jnp.bfloat16)
            for part in range(CHUNK // LANES):
                piece = act[:, part * LANES : (part + 1) * LANES]
                squares = squares + piece * piece
        if layer < layers - 1:
            send_rows(raw, layer + 1)
        mean = jnp.sum(squares, axis=1, keepdims=True) * (1.0 / width)
        norm = lax.rsqrt(mean + 1e-05)
        result = out_ref if layer == layers - 1 else hid
        for c in range(width // CHUNK):
            cols = slice(c * CHUNK, (c + 1) * CHUNK)
            result[:, cols] = (base[:, cols] * norm).astype(jnp.bfloat16)

    sent_all(0, req_send, req_recv)
    for layer in range(layers):
        sent_all(1 + layer, row_send.at[layer], row_recv.at[layer])


def shards(features, w_self, w_neigh, requests, counts, mask_remote, mask_local):
    n = lax.axis_size("rows")
    nodes, width = features.shape
    layers = w_self.shape[0]
    slots = requests.shape[1]
    fetched = n * slots
    flops = 2 * layers * nodes * width * (2 * width + nodes + fetched)
    hbm = pl.BlockSpec(memory_space=pltpu.HBM)
    return pl.pallas_call(
        functools.partial(kernel, n, layers),
        out_shape=pltpu.VMEM((nodes, width), jnp.bfloat16),
        in_specs=[hbm] * 7,
        out_specs=pl.BlockSpec(memory_space=pltpu.VMEM),
        scratch_shapes=[
            pltpu.VMEM((slots, n), jnp.int32),
            pltpu.SMEM(counts.shape, jnp.int32),
            pltpu.VMEM((nodes, width), jnp.bfloat16),
            pltpu.VMEM(w_self.shape, jnp.bfloat16),
            pltpu.VMEM(w_neigh.shape, jnp.bfloat16),
            pltpu.VMEM(mask_remote.shape, jnp.int32),
            pltpu.VMEM(mask_local.shape, jnp.int32),
            pltpu.VMEM((n, 1, LANES), jnp.int32),
            pltpu.VMEM((n, 1, LANES), jnp.int32),
            pltpu.VMEM((layers, n, 2 * slots, width // 2), jnp.bfloat16),
            pltpu.VMEM((layers, n, 2 * slots, width // 2), jnp.bfloat16),
            pltpu.VMEM((nodes, nodes), jnp.bfloat16),
            pltpu.VMEM((nodes, fetched), jnp.bfloat16),
            pltpu.VMEM((fetched, nodes), jnp.bfloat16),
            pltpu.VMEM((nodes, LANES), jnp.float32),
            pltpu.VMEM((nodes, width), jnp.float32),
            pltpu.VMEM((nodes, width), jnp.bfloat16),
            pltpu.SemaphoreType.DMA((5 + 2 * layers,)),
            pltpu.SemaphoreType.DMA((1 + layers, n)),
            pltpu.SemaphoreType.DMA((1 + layers, n)),
        ],
        compiler_params=pltpu.CompilerParams(
            collective_id=0, has_side_effects=True, vmem_limit_bytes=56 * 1024 * 1024
        ),
        cost_estimate=pl.CostEstimate(
            flops=flops, bytes_accessed=8 * width * width + 4 * nodes * width, transcendentals=0
        ),
    )(features, w_self, w_neigh, requests.T, counts, mask_remote, mask_local)


def solution(mesh):
    in_specs = (
        P(("parts", "rows"), None),
        P(),
        P(),
        P(("parts", "rows"), None),
        P(("parts", "rows")),
        P(("parts", "rows"), None),
        P(("parts", "rows"), None),
    )
    out_specs = P(("parts", "rows"), None)
    return jax.shard_map(shards, mesh=mesh, in_specs=in_specs, out_specs=out_specs, check_vma=False)
```
